32 devices in a mesh: groups: 2 (over y), tm: 8 (over z, x), head: 2 (over core).
Axes of the slice: x: 2, y: 2, z: 4, core: 2. Of those that a mesh axis runs over, the one named last changes fastest.
Arguments:
- queries: bfloat16 [1536, 2560], P(('groups', 'tm'), 'head'), parts along dimension 0, may hold values from -1000 to 1000
- keys: bfloat16 [1536, 2560], P(('groups', 'tm'), 'head'), parts along dimension 0, may hold values from -1000 to 1000
- values: bfloat16 [1536, 2560], P(('groups', 'tm'), 'head'), parts along dimension 0, may hold values from -6 to 6
- q_gain: float32 [2560], P('head'), may hold values from 1 to 2
- k_gain: float32 [2560], P('head'), may hold values from 1 to 2
- frames: int32 [16], P(('groups', 'tm')), parts along dimension 0, may hold values from 1 to 3
- flags: int32 [16, 2], P(('groups', 'tm')), parts along dimension 0, may hold values 0 or 1
Outputs:
- attended: bfloat16 [1536, 2560], P(('groups', 'tm'), 'head'), parts along dimension 0
The draws below stay inside these ranges and needn't reach their ends.
There are 2 independent parts, one for each index of `groups`. The reference program is written for one: setup_inputs(seed, part) draws one part's arguments, and reference() takes and returns one part's arrays. A program takes and returns all parts, laid end to end along the dimension named above; an argument that names none is the same for every part. Nothing has to cross between parts.
All inputs are finite; a program needn't handle non-finite values. No bound on the sum of `flags` on one device may be relied on, other than what follows from the above.
Results may differ from the reference program's by a relative error of at most 0.011.
Values may be sent and summed in bfloat16 or wider, within the bound.
A program may use at most 128 MiB of HBM per device.

```python
import math
import jax
import jax.numpy as jnp
from jax import lax

HD = 128
HEADS = 20
FT = 32
F_C = 3
COLS = 2560
T_C = 96
WIN = 64
SPANS = 8
TOKENS = 768


def query_key_fields(key):
    parts = jax.random.split(key, 6)
    tilt = math.sqrt(3.0)
    column_index = jnp.arange(COLS)
    upper_half = jnp.where(column_index >= COLS // 2, tilt, 1.0)
    row_top = 10.0

    def one_field(noise_key, row_key, column_key):
        base = jnp.clip(jax.random.normal(noise_key, (TOKENS, COLS)), -4.0, 4.0)
        row_scale = jnp.exp(jax.random.uniform(row_key, (TOKENS, 1)) * math.log(row_top))
        column_scale = jnp.exp(jax.random.uniform(column_key, (1, COLS)) * math.log(10.0))
        return base * row_scale * column_scale * upper_half[None, :]
    query_field = one_field(parts[0], parts[2], parts[4])
    key_field = one_field(parts[1], parts[3], parts[5])
    return (query_field, key_field)


def draw_queries(key, part):
    return query_key_fields(key)[0].astype(jnp.bfloat16)


def draw_keys(key, part):
    return query_key_fields(key)[1].astype(jnp.bfloat16)


def plant(values, key, least, largest):
    dims = values.shape
    spot = [jax.random.randint(jax.random.fold_in(key, axis), (), 0, dims[axis]) for axis in range(len(dims))]
    values = values.at[tuple(spot)].set(least)
    longest = dims.index(max(dims))
    spot[longest] = (spot[longest] + 1) % dims[longest]
    return values.at[tuple(spot)].set(largest)


def steps_of(own_key, shape, cuts, least, largest):
    level = 1.0
    for position, blocks in cuts:
        steps = jax.random.uniform(jax.random.fold_in(jax.random.fold_in(own_key, 6), position), (blocks,), jnp.float32, least / len(cuts), largest / len(cuts))
        level = level * jnp.repeat(jnp.exp(steps), shape[position] // blocks).reshape((-1,) + (1,) * (len(shape) - 1 - position))
    return level


def gaussian(key, dims, deviation, limit, shards=(), kind=jnp.bfloat16):
    values = deviation * jax.random.normal(key, dims, jnp.float32)
    if shards:
        values = values * steps_of(key, dims, shards, -0.22, 0.18)
    return jnp.clip(values, -limit, limit).astype(kind)


def setup_inputs(seed: int = 0, part: int = 0) -> dict:
    streams_of = jax.random.split(jax.random.key(seed), 8)
    part_splits = jax.random.split(jax.random.fold_in(streams_of[7], part), 8)
    return {
        "queries": draw_queries(jax.random.fold_in(jax.random.fold_in(streams_of[7], part), 71), part),
        "keys": draw_keys(jax.random.fold_in(jax.random.fold_in(streams_of[7], part), 71), part),
        "values": gaussian(part_splits[2], (TOKENS, COLS), 1.0, 6.0, ((0, 8), (1, 2))),
        "q_gain": jnp.clip(1.0 + 1.0 * jax.random.uniform(streams_of[3], (COLS,), jnp.float32) ** steps_of(streams_of[3], (COLS,), ((0, 2),), -0.2, 0.2), 1.0, 2.0),
        "k_gain": jnp.clip(1.0 + 1.0 * jax.random.uniform(streams_of[4], (COLS,), jnp.float32) ** steps_of(streams_of[4], (COLS,), ((0, 2),), -0.2, 0.2), 1.0, 2.0),
        "frames": plant(jax.random.randint(part_splits[5], (SPANS,), 1, F_C + 1), jax.random.fold_in(part_splits[5], 1), 1, F_C).astype(jnp.int32),
        "flags": plant((jax.random.randint(part_splits[6], (SPANS, 2), 0, 4) < 3).astype(jnp.int32), jax.random.fold_in(part_splits[6], 1), 0, 1),
    }


EPSILON = 1e-06

def rms_rows(inputs, gain):
    widened = inputs.astype(jnp.float32)
    level = lax.optimization_barrier(jnp.mean(widened * widened, axis=1, keepdims=True))
    return (widened * lax.rsqrt(level + EPSILON) * gain).astype(jnp.bfloat16)

def reference(queries, keys, values, q_gain, k_gain, frames, flags):
    q_norm = rms_rows(queries, q_gain).reshape(SPANS, T_C, HEADS, HD)
    k_norm = rms_rows(keys, k_gain).reshape(SPANS, T_C, HEADS, HD)
    value_all = values.reshape(SPANS, T_C, HEADS, HD)
    counts = frames.astype(jnp.int32) * FT
    sink_keys = k_norm[0, :FT]
    sink_values = value_all[0, :FT]
    slot_index = jnp.arange(T_C, dtype=jnp.int32)
    scaling = 1.0 / math.sqrt(HD)

    def one_span(span_index):
        before = jnp.maximum(span_index - 1, 0).astype(jnp.int32)
        earlier = jnp.maximum(span_index - 2, 0).astype(jnp.int32)
        n_current = counts[span_index]
        n_before = jnp.where(span_index >= 1, counts[before], 0).astype(jnp.int32)
        n_earlier = jnp.where(span_index >= 2, counts[earlier], 0).astype(jnp.int32)
        use_sink = flags[span_index, 0] > 0
        use_window = flags[span_index, 1] > 0
        key_set = jnp.concatenate([sink_keys, k_norm[earlier], k_norm[before], k_norm[span_index]], 0)
        value_set = jnp.concatenate([sink_values, value_all[earlier], value_all[before], value_all[span_index]], 0)
        allowed = jnp.concatenate([jnp.full((FT,), use_sink), use_window & (slot_index < n_earlier) & (slot_index >= n_before + n_earlier - WIN), use_window & (slot_index < n_before) & (slot_index >= n_before - WIN), slot_index < n_current])
        query_rows = q_norm[span_index].astype(jnp.float32)
        score = jnp.einsum('qhd,khd->hqk', query_rows, key_set.astype(jnp.float32)) * scaling
        score = jnp.where(allowed[None, None, :], score, -jnp.inf)
        highest = lax.optimization_barrier(jnp.max(score, axis=2, keepdims=True))
        weight = jnp.exp(score - highest).astype(jnp.bfloat16)
        denominator = lax.optimization_barrier(jnp.sum(weight.astype(jnp.float32), axis=2))
        blended = jnp.einsum('hqk,khd->qhd', weight.astype(jnp.float32), value_set.astype(jnp.float32))
        blended = blended / jnp.transpose(denominator)[:, :, None]
        blended = jnp.where((slot_index < n_current)[:, None, None], blended, 0.0)
        return blended.astype(jnp.bfloat16)
    span_blocks = lax.map(one_span, jnp.arange(SPANS, dtype=jnp.int32))
    return span_blocks.reshape(TOKENS, COLS)
```

```python
import functools
import math

import jax
import jax.numpy as jnp
from jax import lax
from jax.experimental import pallas as pl
from jax.experimental.pallas import tpu as pltpu
from jax.sharding import PartitionSpec as P

HD = 128
FT = 32
EPSILON = 1e-06
MASKED = -1e30

ENERGY, COUNT, V_NEW, K_NEW, V_OLD, K_OLD, V_SINK, K_SINK = range(8)


def kernel(spans, heads_axis, q_hbm, k_hbm, v_hbm, q_gain, k_gain, frames, flags, out,
           q_raw, k_raw, q_norm, k_all, v_all, energy, energy_in, count, count_in,
           v_new, k_new, v_old, k_old, own_max, own_sum, own_out,
           local_sem, send_sem, recv_sem, hop_sem):
    rows, cols = q_hbm.shape
    heads = cols // HD
    window = 2 * FT
    older, newer, sink = rows, rows + FT, rows + window
    full_width = cols * heads_axis
    t = lax.axis_index("tm")
    side = lax.axis_index("head")
    even = t % 2 == 0

    def column(h):
        return pl.ds(h * HD, HD)

    def load(source, target, index):
        return pltpu.make_async_copy(source, target, local_sem.at[index])

    loads = [load(k_hbm, k_raw, 0), load(q_hbm, q_raw, 1), load(v_hbm, v_all.at[pl.ds(0, rows)], 2)]
    for copy in loads:
        copy.start()

    barrier = pltpu.get_barrier_semaphore()

    def greet(condition, **where):
        @pl.when(condition)
        def _():
            pl.semaphore_signal(barrier, inc=1, device_id=where, device_id_type=pl.DeviceIdType.MESH)

    for other in range(1, heads_axis):
        greet(side >= 0, head=lax.rem(side + other, heads_axis))
    partners = heads_axis - 1
    for step in (-2, -1, 1, 2):
        there = (t + step >= 0) & (t + step < spans)
        greet(there, tm=t + step)
        partners = partners + there.astype(jnp.int32)

    n = frames[0] * FT

    @pl.when(t == 0)
    def _():
        blank = jnp.zeros((window, cols), jnp.bfloat16)
        k_all[pl.ds(older, window)] = blank
        v_all[pl.ds(older, window)] = blank
        count_in[...] = jnp.zeros_like(count_in)

    count[...] = jnp.full(count.shape, n, jnp.int32)

    def remote(kind, source, target, sem=None, **where):
        return pltpu.make_async_remote_copy(
            src_ref=source, dst_ref=target,
            send_sem=send_sem.at[kind] if sem is None else sem, recv_sem=recv_sem.at[kind],
            device_id=where, device_id_type=pl.DeviceIdType.MESH)

    after = {"tm": jnp.minimum(t + 1, spans - 1)}
    before = {"tm": jnp.maximum(t - 1, 0)}
    hop = {"tm": jnp.minimum(t + 2, spans - 1)}
    has_after = t + 1 < spans
    has_hop = t + 2 < spans

    def squares(ref):
        total = jnp.zeros((rows, HD), jnp.float32)
        for h in range(heads):
            block = ref[:, column(h)].astype(jnp.float32)
            total = total + block * block
        return total

    loads[0].wait()
    energy[0] = squares(k_raw)
    loads[1].wait()
    energy[1] = squares(q_raw)

    pl.semaphore_wait(barrier, partners)
    share = remote(ENERGY, energy, energy_in, head=lax.rem(side + 1, heads_axis))
    share.start()

    loads[2].wait()

    def newest(source, target):
        for h in range(heads):
            a, b, c = (source[pl.ds(i * FT, FT), column(h)] for i in range(3))
            target[:, column(h)] = jnp.where(n >= 3 * FT, c, jnp.where(n >= 2 * FT, b, a))

    def second(source, target):
        for h in range(heads):
            a, b = (source[pl.ds(i * FT, FT), column(h)] for i in range(2))
            got = source[pl.ds(newer, FT), column(h)]
            target[:, column(h)] = jnp.where(n >= 3 * FT, b, jnp.where(n >= 2 * FT, a, got))

    counts = remote(COUNT, count, count_in, **after)
    sends = {
        V_NEW: remote(V_NEW, v_new, v_all.at[pl.ds(newer, FT)], **after),
        K_NEW: remote(K_NEW, k_new, k_all.at[pl.ds(newer, FT)], **after),
        V_OLD: remote(V_OLD, v_old, v_all.at[pl.ds(older, FT)], **after),
        K_OLD: remote(K_OLD, k_old, k_all.at[pl.ds(older, FT)], **after),
    }

    def sink_sends(kind, ref):
        at = ref.at[pl.ds(sink, FT)]
        along = remote(kind, at, at, sem=hop_sem.at[kind - V_SINK], **hop)
        across = remote(kind, at, at, **after)
        return along, across

    def sink_pass(kind, ref):
        along, across = sink_sends(kind, ref)

        @pl.when(even & has_hop)
        def _():
            along.start()

        @pl.when(even & has_after)
        def _():
            across.start()

    def sink_take(kind, ref):
        @pl.when(t > 0)
        def _():
            sink_sends(kind, ref)[1].wait_recv()

    @pl.when(t == 0)
    def _():
        v_all[pl.ds(sink, FT)] = v_all[pl.ds(0, FT)]
        sink_pass(V_SINK, v_all)

    newest(v_all, v_new)

    @pl.when(has_after)
    def _():
        sends[V_NEW].start()
        counts.start()

    share.wait()

    def level(index):
        total = jnp.sum(energy[index] + energy_in[index], axis=1, keepdims=True)
        return lax.rsqrt(total / full_width + EPSILON)

    k_level, q_level = level(0), level(1)
    for h in range(heads):
        k_all[pl.ds(0, rows), column(h)] = (
            k_raw[:, column(h)].astype(jnp.float32) * k_level * k_gain[:, column(h)]
        ).astype(jnp.bfloat16)

    @pl.when(t == 0)
    def _():
        k_all[pl.ds(sink, FT)] = k_all[pl.ds(0, FT)]
        sink_pass(K_SINK, k_all)

    newest(k_all, k_new)

    @pl.when(has_after)
    def _():
        sends[K_NEW].start()

    for h in range(heads):
        q_norm[:, column(h)] = (
            q_raw[:, column(h)].astype(jnp.float32) * q_level * q_gain[:, column(h)]
        ).astype(jnp.bfloat16)

    def received(kind):
        @pl.when(t > 0)
        def _():
            sends[kind].wait_recv()

    scaling = math.log2(math.e) / math.sqrt(HD)

    def scores(h, start, allowed):
        products = lax.dot_general(
            q_norm[:, column(h)], k_all[pl.ds(start, rows), column(h)],
            (((1,), (1,)), ((), ())), preferred_element_type=jnp.float32)
        return jnp.where(allowed, products * scaling, MASKED)

    def mix(weight, h, start):
        return jnp.dot(weight.astype(jnp.bfloat16), v_all[pl.ds(start, rows), column(h)],
                       preferred_element_type=jnp.float32)

    lane = lax.broadcasted_iota(jnp.int32, (1, rows), 1)
    live_keys = lane < n
    live_rows = lax.broadcasted_iota(jnp.int32, (rows, 1), 0) < n

    def own(h):
        s = scores(h, 0, live_keys)
        top = jnp.max(s, axis=1, keepdims=True)
        weight = jnp.exp2(s - top)
        own_max[h] = top
        own_sum[h] = jnp.sum(weight, axis=1, keepdims=True)
        own_out[:, column(h)] = mix(weight, h, 0)

    third = heads // 3
    received(V_NEW)
    second(v_all, v_old)

    @pl.when(has_after)
    def _():
        sends[V_OLD].start()

    for h in range(third):
        own(h)

    received(K_NEW)
    second(k_all, k_old)

    @pl.when(has_after)
    def _():
        sends[K_OLD].start()

    sink_take(V_SINK, v_all)

    @pl.when(t > 0)
    def _():
        sink_pass(V_SINK, v_all)

    for h in range(third, 2 * third):
        own(h)
    sink_take(K_SINK, k_all)

    @pl.when(t > 0)
    def _():
        sink_pass(K_SINK, k_all)

    for h in range(2 * third, heads):
        own(h)

    @pl.when(t > 0)
    def _():
        counts.wait_recv()

    received(V_OLD)
    received(K_OLD)

    use_sink = flags[0, 0]
    use_window = flags[0, 1]
    held = jnp.where(t >= 2, window, count_in[0:1, :rows])
    allowed = jnp.where(
        lane >= window, use_sink,
        use_window * jnp.where(lane >= FT, (held > 0).astype(jnp.int32),
                               (held >= window).astype(jnp.int32))) > 0

    for h in range(heads):
        s = scores(h, older, allowed)
        top = jnp.maximum(jnp.max(s, axis=1, keepdims=True), own_max[h])
        weight = jnp.exp2(s - top)
        keep = jnp.exp2(own_max[h] - top)
        denominator = jnp.sum(weight, axis=1, keepdims=True) + own_sum[h] * keep
        total = mix(weight, h, older) + own_out[:, column(h)] * keep
        out[:, column(h)] = jnp.where(live_rows, total / denominator, 0.0).astype(jnp.bfloat16)

    @pl.when(has_after)
    def _():
        counts.wait_send()
        for copy in sends.values():
            copy.wait_send()

    for kind, ref in ((V_SINK, v_all), (K_SINK, k_all)):
        along, across = sink_sends(kind, ref)

        @pl.when(even & has_hop)
        def _():
            along.wait_send()

        @pl.when(even & has_after)
        def _():
            across.wait_send()


def local(spans, heads_axis, queries, keys, values, q_gain, k_gain, frames, flags):
    rows, cols = queries.shape
    heads = cols // HD
    far = pl.BlockSpec(memory_space=pl.ANY)
    near = pl.BlockSpec(memory_space=pltpu.VMEM)
    scalar = pl.BlockSpec(memory_space=pltpu.SMEM)
    bf16, f32 = jnp.bfloat16, jnp.float32
    held = 2 * rows
    return pl.pallas_call(
        functools.partial(kernel, spans, heads_axis),
        out_shape=jax.ShapeDtypeStruct((rows, cols), bf16),
        in_specs=[far, far, far, near, near, scalar, scalar],
        out_specs=near,
        scratch_shapes=[
            pltpu.VMEM((rows, cols), bf16),
            pltpu.VMEM((rows, cols), bf16),
            pltpu.VMEM((rows, cols), bf16),
            pltpu.VMEM((held, cols), bf16),
            pltpu.VMEM((held, cols), bf16),
            pltpu.VMEM((2, rows, HD), f32),
            pltpu.VMEM((2, rows, HD), f32),
            pltpu.VMEM((8, HD), jnp.int32),
            pltpu.VMEM((8, HD), jnp.int32),
            pltpu.VMEM((FT, cols), bf16),
            pltpu.VMEM((FT, cols), bf16),
            pltpu.VMEM((FT, cols), bf16),
            pltpu.VMEM((FT, cols), bf16),
            pltpu.VMEM((heads, rows, 1), f32),
            pltpu.VMEM((heads, rows, 1), f32),
            pltpu.VMEM((rows, cols), f32),
            pltpu.SemaphoreType.DMA((3,)),
            pltpu.SemaphoreType.DMA((8,)),
            pltpu.SemaphoreType.DMA((8,)),
            pltpu.SemaphoreType.DMA((2,)),
        ],
        compiler_params=pltpu.CompilerParams(
            collective_id=0, has_side_effects=True, vmem_limit_bytes=32 * 2**20),
    )(queries, keys, values, q_gain.reshape(1, cols), k_gain.reshape(1, cols), frames, flags)


def solution(mesh):
    placed = (
        P(("groups", "tm"), "head"),
        P(("groups", "tm"), "head"),
        P(("groups", "tm"), "head"),
        P("head"),
        P("head"),
        P(("groups", "tm")),
        P(("groups", "tm"), None),
    )
    return jax.shard_map(
        functools.partial(local, mesh.shape["tm"], mesh.shape["head"]),
        mesh=mesh, in_specs=placed, out_specs=P(("groups", "tm"), "head"), check_vma=False
    )
```

```python
import functools
import math

import jax
import jax.numpy as jnp
from jax import lax
from jax.experimental import pallas as pl
from jax.experimental.pallas import tpu as pltpu
from jax.sharding import PartitionSpec as P

HD = 128
FT = 32
EPSILON = 1e-06
MASKED = -1e30

PIECES = 2
CROSSING = (0, 1, 2, 3)
K_ENERGY, Q_ENERGY, COUNT, V_NEW, K_NEW, V_OLD, K_OLD, V_SINK = range(8)
K_SINK = V_SINK + PIECES
COPIES = K_SINK + PIECES


def kernel(spans, heads_axis, q_hbm, k_hbm, v_hbm, q_gain_hbm, k_gain_hbm, frames_hbm, flags_hbm, out,
           q_gain, k_gain, frames, flags, q_raw, k_raw, q_norm, k_all, v_all, energy, energy_in, count, count_in,
           v_new, k_new, v_old, k_old, own_max, own_sum, own_out,
           local_sem, send_sem, recv_sem, hop_sem):
    rows, cols = q_hbm.shape
    heads = cols // HD
    window = 2 * FT
    older, newer, sink = rows, rows + FT, rows + window
    full_width = cols * heads_axis
    t = lax.axis_index("tm")
    even = t % 2 == 0
    side = lax.axis_index("head")

    def column(h):
        return pl.ds(h * HD, HD)

    def load(source, target, index):
        return pltpu.make_async_copy(source, target, local_sem.at[index])

    loads = [load(k_hbm, k_raw, 0), load(v_hbm, v_all.at[pl.ds(0, rows)], 1),
             load(frames_hbm, frames, 2), load(flags_hbm, flags, 3), load(k_gain_hbm, k_gain, 4),
             load(q_hbm, q_raw, 5), load(q_gain_hbm, q_gain, 6)]
    for copy in loads:
        copy.start()

    barrier = pltpu.get_barrier_semaphore()

    def greet(condition, **where):
        @pl.when(condition)
        def _():
            pl.semaphore_signal(barrier, inc=1, device_id=where, device_id_type=pl.DeviceIdType.MESH)

    for other in range(1, heads_axis):
        greet(side >= 0, head=lax.rem(side + other, heads_axis))
    partners = heads_axis - 1
    for step in (-2, -1, 1, 2):
        there = (t + step >= 0) & (t + step < spans)
        greet(there, tm=t + step)
        partners = partners + there.astype(jnp.int32)

    @pl.when(t == 0)
    def _():
        blank = jnp.zeros((window, cols), jnp.bfloat16)
        k_all[pl.ds(older, window)] = blank
        v_all[pl.ds(older, window)] = blank
        count_in[...] = jnp.zeros_like(count_in)

    def remote(kind, source, target, sem=None, **where):
        return pltpu.make_async_remote_copy(
            src_ref=source, dst_ref=target,
            send_sem=send_sem.at[kind] if sem is None else sem, recv_sem=recv_sem.at[kind],
            device_id=where, device_id_type=pl.DeviceIdType.MESH)

    after = {"tm": jnp.minimum(t + 1, spans - 1)}
    hop = {"tm": jnp.minimum(t + 2, spans - 1)}
    has_after = t + 1 < spans
    has_hop = t + 2 < spans

    def squares(ref):
        total = jnp.zeros((rows, HD), jnp.float32)
        for h in range(heads):
            block = ref[:, column(h)].astype(jnp.float32)
            total = total + block * block
        return total

    def piece(i):
        first, last = heads * i // PIECES, heads * (i + 1) // PIECES
        return pl.ds(first * HD, (last - first) * HD)

    def sink_sends(kind, ref, i):
        at = ref.at[pl.ds(sink, FT), piece(i)]
        index = kind - V_SINK + i
        along = remote(kind + i, at, at, sem=hop_sem.at[index], **hop)
        across = remote(kind + i, at, at, **after)
        return along, across

    def sink_goes(kind, i):
        if kind - V_SINK + i in CROSSING:
            return even & has_hop, even & has_after
        return has_hop, (t == 0) & has_after

    def sink_pass(kind, ref, i):
        along, across = sink_sends(kind, ref, i)
        goes_along, goes_across = sink_goes(kind, i)

        @pl.when(goes_along)
        def _():
            along.start()

        @pl.when(goes_across)
        def _():
            across.start()

    def sink_take(kind, ref, i):
        @pl.when(t > 0)
        def _():
            sink_sends(kind, ref, i)[1].wait_recv()
            sink_pass(kind, ref, i)

    def newest(source, target):
        for h in range(heads):
            a, b, c = (source[pl.ds(i * FT, FT), column(h)] for i in range(3))
            target[:, column(h)] = jnp.where(n >= 3 * FT, c, jnp.where(n >= 2 * FT, b, a))

    def second(source, target):
        for h in range(heads):
            a, b = (source[pl.ds(i * FT, FT), column(h)] for i in range(2))
            got = source[pl.ds(newer, FT), column(h)]
            target[:, column(h)] = jnp.where(n >= 3 * FT, b, jnp.where(n >= 2 * FT, a, got))

    counts = remote(COUNT, count, count_in, **after)
    sends = {
        V_NEW: remote(V_NEW, v_new, v_all.at[pl.ds(newer, FT)], **after),
        K_NEW: remote(K_NEW, k_new, k_all.at[pl.ds(newer, FT)], **after),
        V_OLD: remote(V_OLD, v_old, v_all.at[pl.ds(older, FT)], **after),
        K_OLD: remote(K_OLD, k_old, k_all.at[pl.ds(older, FT)], **after),
    }
    shares = [remote(kind, energy.at[kind], energy_in.at[kind], head=lax.rem(side + 1, heads_axis))
              for kind in (K_ENERGY, Q_ENERGY)]

    for copy in loads[:5]:
        copy.wait()
    n = frames[0] * FT
    count[...] = jnp.full(count.shape, n, jnp.int32)
    energy[K_ENERGY] = squares(k_raw)
    newest(v_all, v_new)

    @pl.when(t == 0)
    def _():
        v_all[pl.ds(sink, FT)] = v_all[pl.ds(0, FT)]

    pl.semaphore_wait(barrier, partners)
    shares[K_ENERGY].start()

    @pl.when(t == 0)
    def _():
        for i in range(PIECES):
            sink_pass(V_SINK, v_all, i)

    @pl.when(has_after)
    def _():
        sends[V_NEW].start()
        counts.start()

    for copy in loads[5:]:
        copy.wait()
    energy[Q_ENERGY] = squares(q_raw)
    shares[Q_ENERGY].start()

    def level(index):
        shares[index].wait()
        total = jnp.sum(energy[index] + energy_in[index], axis=1, keepdims=True)
        return lax.rsqrt(total / full_width + EPSILON)

    k_level = level(K_ENERGY)
    for h in range(heads):
        k_all[pl.ds(0, rows), column(h)] = (
            k_raw[:, column(h)].astype(jnp.float32) * k_level * k_gain[column(h)].reshape(1, HD)
        ).astype(jnp.bfloat16)

    @pl.when(t == 0)
    def _():
        k_all[pl.ds(sink, FT)] = k_all[pl.ds(0, FT)]
        for i in range(PIECES):
            sink_pass(K_SINK, k_all, i)

    newest(k_all, k_new)

    @pl.when(has_after)
    def _():
        sends[K_NEW].start()

    q_level = level(Q_ENERGY)
    for h in range(heads):
        q_norm[:, column(h)] = (
            q_raw[:, column(h)].astype(jnp.float32) * q_level * q_gain[column(h)].reshape(1, HD)
        ).astype(jnp.bfloat16)

    def received(kind):
        @pl.when(t > 0)
        def _():
            sends[kind].wait_recv()

    scaling = math.log2(math.e) / math.sqrt(HD)

    def scores(h, start, allowed):
        products = lax.dot_general(
            q_norm[:, column(h)], k_all[pl.ds(start, rows), column(h)],
            (((1,), (1,)), ((), ())), preferred_element_type=jnp.float32)
        return jnp.where(allowed, products * scaling, MASKED)

    def mix(weight, h, start):
        return jnp.dot(weight, v_all[pl.ds(start, rows), column(h)],
                       preferred_element_type=jnp.float32)

    ones = jnp.ones((rows, HD), jnp.bfloat16)

    def total_of(weight):
        return jnp.dot(weight, ones, preferred_element_type=jnp.float32)

    lane = lax.broadcasted_iota(jnp.int32, (1, rows), 1)
    live_keys = lane < n
    live_rows = lax.broadcasted_iota(jnp.int32, (rows, 1), 0) < n

    def own(h):
        s = scores(h, 0, live_keys)
        top = jnp.max(s, axis=1, keepdims=True)
        weight = jnp.exp2(s - top)
        own_max[h] = top
        weight = weight.astype(jnp.bfloat16)
        own_sum[:, column(h)] = total_of(weight)
        own_out[:, column(h)] = mix(weight, h, 0)

    received(V_NEW)
    second(v_all, v_old)

    @pl.when(has_after)
    def _():
        sends[V_OLD].start()

    received(K_NEW)
    second(k_all, k_old)

    @pl.when(has_after)
    def _():
        sends[K_OLD].start()

    stages = 2 * PIECES
    for stage in range(stages):
        if stage < PIECES:
            sink_take(V_SINK, v_all, stage)
        else:
            sink_take(K_SINK, k_all, stage - PIECES)
        for h in range(heads * stage // stages, heads * (stage + 1) // stages):
            own(h)

    @pl.when(t > 0)
    def _():
        counts.wait_recv()

    received(V_OLD)
    received(K_OLD)

    use_sink = flags[0, 0]
    use_window = flags[0, 1]
    held = jnp.where(t >= 2, window, count_in[0:1, :rows])
    allowed = jnp.where(
        lane >= window, use_sink,
        use_window * jnp.where(lane >= FT, (held > 0).astype(jnp.int32),
                               (held >= window).astype(jnp.int32))) > 0

    for h in range(heads):
        s = scores(h, older, allowed)
        top = jnp.maximum(jnp.max(s, axis=1, keepdims=True), own_max[h])
        weight = jnp.exp2(s - top).astype(jnp.bfloat16)
        keep = jnp.exp2(own_max[h] - top)
        denominator = total_of(weight) + own_sum[:, column(h)] * keep
        total = mix(weight, h, older) + own_out[:, column(h)] * keep
        out[:, column(h)] = jnp.where(live_rows, total / denominator, 0.0).astype(jnp.bfloat16)

    @pl.when(has_after)
    def _():
        counts.wait_send()
        for copy in sends.values():
            copy.wait_send()

    for kind, ref in ((V_SINK, v_all), (K_SINK, k_all)):
        for i in range(PIECES):
            along, across = sink_sends(kind, ref, i)
            goes_along, goes_across = sink_goes(kind, i)

            @pl.when(goes_along)
            def _():
                along.wait_send()

            @pl.when(goes_across)
            def _():
                across.wait_send()


def local(spans, heads_axis, queries, keys, values, q_gain, k_gain, frames, flags):
    rows, cols = queries.shape
    heads = cols // HD
    far = pl.BlockSpec(memory_space=pltpu.HBM)
    near = pl.BlockSpec(memory_space=pltpu.VMEM)
    bf16, f32 = jnp.bfloat16, jnp.float32
    held = 2 * rows
    return pl.pallas_call(
        functools.partial(kernel, spans, heads_axis),
        out_shape=pltpu.VMEM((rows, cols), bf16),
        in_specs=[far] * 7,
        out_specs=near,
        scratch_shapes=[
            pltpu.VMEM((cols,), f32),
            pltpu.VMEM((cols,), f32),
            pltpu.SMEM(frames.shape, jnp.int32),
            pltpu.SMEM(flags.shape, jnp.int32),
            pltpu.VMEM((rows, cols), bf16),
            pltpu.VMEM((rows, cols), bf16),
            pltpu.VMEM((rows, cols), bf16),
            pltpu.VMEM((held, cols), bf16),
            pltpu.VMEM((held, cols), bf16),
            pltpu.VMEM((2, rows, HD), f32),
            pltpu.VMEM((2, rows, HD), f32),
            pltpu.VMEM((8, HD), jnp.int32),
            pltpu.VMEM((8, HD), jnp.int32),
            pltpu.VMEM((FT, cols), bf16),
            pltpu.VMEM((FT, cols), bf16),
            pltpu.VMEM((FT, cols), bf16),
            pltpu.VMEM((FT, cols), bf16),
            pltpu.VMEM((heads, rows, 1), f32),
            pltpu.VMEM((rows, cols), f32),
            pltpu.VMEM((rows, cols), f32),
            pltpu.SemaphoreType.DMA((7,)),
            pltpu.SemaphoreType.DMA((COPIES,)),
            pltpu.SemaphoreType.DMA((COPIES,)),
            pltpu.SemaphoreType.DMA((2 * PIECES,)),
        ],
        compiler_params=pltpu.CompilerParams(
            collective_id=0, has_side_effects=True, vmem_limit_bytes=63 * 2**20),
    )(queries, keys, values, q_gain, k_gain, frames, flags)


def solution(mesh):
    placed = (
        P(("groups", "tm"), "head"),
        P(("groups", "tm"), "head"),
        P(("groups", "tm"), "head"),
        P("head"),
        P("head"),
        P(("groups", "tm")),
        P(("groups", "tm"), None),
    )
    return jax.shard_map(
        functools.partial(local, mesh.shape["tm"], mesh.shape["head"]),
        mesh=mesh, in_specs=placed, out_specs=P(("groups", "tm"), "head"), check_vma=False
    )
```

```python
import functools
import math

import jax
import jax.numpy as jnp
from jax import lax
from jax.experimental import pallas as pl
from jax.experimental.pallas import tpu as pltpu
from jax.sharding import PartitionSpec as P

HD = 128
FT = 32
EPSILON = 1e-06
MASKED = -1e30

PIECES = 2
CROSSING = (0, 1, 2, 3)
K_ENERGY, Q_ENERGY, COUNT, V_NEW, K_NEW, V_OLD, K_OLD, V_SINK = range(8)
K_SINK = V_SINK + PIECES
COPIES = K_SINK + PIECES


def kernel(spans, heads_axis, q_hbm, k_hbm, v_hbm, q_gain_hbm, k_gain_hbm, frames_hbm, flags_hbm, out,
           q_gain, k_gain, frames, flags, q_raw, k_raw, q_norm, k_all, v_all, energy, energy_in, count, count_in,
           v_new, k_new, v_old, k_old, own_max, own_sum, own_out,
           local_sem, send_sem, recv_sem, hop_sem):
    rows, cols = q_hbm.shape
    heads = cols // HD
    window = 2 * FT
    older, newer, sink = rows, rows + FT, rows + window
    full_width = cols * heads_axis
    t = lax.axis_index("tm")
    even = t % 2 == 0
    side = lax.axis_index("head")

    def column(h):
        return pl.ds(h * HD, HD)

    def load(source, target, index):
        return pltpu.make_async_copy(source, target, local_sem.at[index])

    loads = [load(k_hbm, k_raw, 0), load(v_hbm, v_all.at[pl.ds(0, rows)], 1),
             load(frames_hbm, frames, 2), load(flags_hbm, flags, 3), load(k_gain_hbm, k_gain, 4),
             load(q_hbm, q_raw, 5), load(q_gain_hbm, q_gain, 6)]
    for copy in loads:
        copy.start()

    barrier = pltpu.get_barrier_semaphore()

    def greet(condition, **where):
        @pl.when(condition)
        def _():
            pl.semaphore_signal(barrier, inc=1, device_id=where, device_id_type=pl.DeviceIdType.MESH)

    for other in range(1, heads_axis):
        greet(side >= 0, head=lax.rem(side + other, heads_axis))
    partners = heads_axis - 1
    for step in (-2, -1, 1, 2):
        there = (t + step >= 0) & (t + step < spans)
        greet(there, tm=t + step)
        partners = partners + there.astype(jnp.int32)

    @pl.when(t == 0)
    def _():
        blank = jnp.zeros((window, cols), jnp.bfloat16)
        k_all[pl.ds(older, window)] = blank
        v_all[pl.ds(older, window)] = blank
        count_in[...] = jnp.zeros_like(count_in)

    def remote(kind, source, target, sem=None, **where):
        return pltpu.make_async_remote_copy(
            src_ref=source, dst_ref=target,
            send_sem=send_sem.at[kind] if sem is None else sem, recv_sem=recv_sem.at[kind],
            device_id=where, device_id_type=pl.DeviceIdType.MESH)

    after = {"tm": jnp.minimum(t + 1, spans - 1)}
    hop = {"tm": jnp.minimum(t + 2, spans - 1)}
    has_after = t + 1 < spans
    has_hop = t + 2 < spans

    def squares(ref):
        total = jnp.zeros((rows, HD), jnp.float32)
        for h in range(heads):
            block = ref[:, column(h)].astype(jnp.float32)
            total = total + block * block
        return total

    def piece(i):
        first, last = heads * i // PIECES, heads * (i + 1) // PIECES
        return pl.ds(first * HD, (last - first) * HD)

    def sink_sends(kind, ref, i):
        at = ref.at[pl.ds(sink, FT), piece(i)]
        index = kind - V_SINK + i
        along = remote(kind + i, at, at, sem=hop_sem.at[index], **hop)
        across = remote(kind + i, at, at, **after)
        return along, across

    def sink_goes(kind, i):
        if kind - V_SINK + i in CROSSING:
            return even & has_hop, even & has_after
        return has_hop, (t == 0) & has_after

    def sink_pass(kind, ref, i):
        along, across = sink_sends(kind, ref, i)
        goes_along, goes_across = sink_goes(kind, i)

        @pl.when(goes_along)
        def _():
            along.start()

        @pl.when(goes_across)
        def _():
            across.start()

    def sink_take(kind, ref, i):
        @pl.when(t > 0)
        def _():
            sink_sends(kind, ref, i)[1].wait_recv()
            sink_pass(kind, ref, i)

    def newest(source, target):
        for h in range(heads):
            a, b, c = (source[pl.ds(i * FT, FT), column(h)] for i in range(3))
            target[:, column(h)] = jnp.where(n >= 3 * FT, c, jnp.where(n >= 2 * FT, b, a))

    def second(source, target):
        for h in range(heads):
            a, b = (source[pl.ds(i * FT, FT), column(h)] for i in range(2))
            got = source[pl.ds(newer, FT), column(h)]
            target[:, column(h)] = jnp.where(n >= 3 * FT, b, jnp.where(n >= 2 * FT, a, got))

    counts = remote(COUNT, count, count_in, **after)
    sends = {
        V_NEW: remote(V_NEW, v_new, v_all.at[pl.ds(newer, FT)], **after),
        K_NEW: remote(K_NEW, k_new, k_all.at[pl.ds(newer, FT)], **after),
        V_OLD: remote(V_OLD, v_old, v_all.at[pl.ds(older, FT)], **after),
        K_OLD: remote(K_OLD, k_old, k_all.at[pl.ds(older, FT)], **after),
    }
    shares = [remote(kind, energy.at[kind], energy_in.at[kind], head=lax.rem(side + 1, heads_axis))
              for kind in (K_ENERGY, Q_ENERGY)]

    for copy in loads[:5]:
        copy.wait()
    n = frames[0] * FT
    count[...] = jnp.full(count.shape, n, jnp.int32)
    energy[K_ENERGY] = squares(k_raw)
    newest(v_all, v_new)

    @pl.when(t == 0)
    def _():
        v_all[pl.ds(sink, FT)] = v_all[pl.ds(0, FT)]

    pl.semaphore_wait(barrier, partners)
    shares[K_ENERGY].start()

    @pl.when(t == 0)
    def _():
        for i in range(PIECES):
            sink_pass(V_SINK, v_all, i)

    @pl.when(has_after)
    def _():
        sends[V_NEW].start()
        counts.start()

    for copy in loads[5:]:
        copy.wait()
    energy[Q_ENERGY] = squares(q_raw)
    shares[Q_ENERGY].start()

    def level(index):
        shares[index].wait()
        total = jnp.sum(energy[index] + energy_in[index], axis=1, keepdims=True)
        return lax.rsqrt(total / full_width + EPSILON)

    k_level = level(K_ENERGY)
    for h in range(heads):
        k_all[pl.ds(0, rows), column(h)] = (
            k_raw[:, column(h)].astype(jnp.float32) * k_level * k_gain[column(h)].reshape(1, HD)
        ).astype(jnp.bfloat16)

    @pl.when(t == 0)
    def _():
        k_all[pl.ds(sink, FT)] = k_all[pl.ds(0, FT)]
        for i in range(PIECES):
            sink_pass(K_SINK, k_all, i)

    newest(k_all, k_new)

    @pl.when(has_after)
    def _():
        sends[K_NEW].start()

    q_level = level(Q_ENERGY)
    for h in range(heads):
        q_norm[:, column(h)] = (
            q_raw[:, column(h)].astype(jnp.float32) * q_level * q_gain[column(h)].reshape(1, HD)
        ).astype(jnp.bfloat16)

    def received(kind):
        @pl.when(t > 0)
        def _():
            sends[kind].wait_recv()

    scaling = math.log2(math.e) / math.sqrt(HD)

    def scores(h, start, allowed):
        products = lax.dot_general(
            q_norm[:, column(h)], k_all[pl.ds(start, rows), column(h)],
            (((1,), (1,)), ((), ())), preferred_element_type=jnp.float32)
        return jnp.where(allowed, products * scaling, MASKED)

    def mix(weight, h, start):
        return jnp.dot(weight, v_all[pl.ds(start, rows), column(h)],
                       preferred_element_type=jnp.float32)

    ones = jnp.ones((rows, HD), jnp.bfloat16)

    def total_of(weight):
        return jnp.dot(weight, ones, preferred_element_type=jnp.float32)

    lane = lax.broadcasted_iota(jnp.int32, (1, rows), 1)
    live_keys = lane < n
    live_rows = lax.broadcasted_iota(jnp.int32, (rows, 1), 0) < n

    def own(h):
        s = scores(h, 0, live_keys)
        top = jnp.max(s, axis=1, keepdims=True)
        weight = jnp.exp2(s - top)
        own_max[h] = top
        weight = weight.astype(jnp.bfloat16)
        own_sum[:, column(h)] = total_of(weight)
        own_out[:, column(h)] = mix(weight, h, 0)

    def hand_on(new, old, ref, scratch):
        received(new)
        second(ref, scratch)

        @pl.when(has_after)
        def _():
            sends[old].start()

    def follow(order):
        done = 0
        for step, (what, ready) in enumerate(order):
            if what == V_NEW:
                hand_on(V_NEW, V_OLD, v_all, v_old)
            elif what == K_NEW:
                hand_on(K_NEW, K_OLD, k_all, k_old)
            elif what < K_SINK:
                sink_take(V_SINK, v_all, what - V_SINK)
            else:
                sink_take(K_SINK, k_all, what - K_SINK)
            for h in range(done, ready):
                own(h)
            done = ready
        assert done == heads

    def spaced(order, counts):
        total = sum(counts)
        return [(what, heads * sum(counts[:i + 1]) // total) for i, what in enumerate(order)]

    v_sinks = [V_SINK + i for i in range(PIECES)]
    k_sinks = [K_SINK + i for i in range(PIECES)]

    @pl.when(even)
    def _():
        follow(spaced(v_sinks + [V_NEW, K_NEW] + k_sinks, [0, 1, 1, 3, 3, 2]))

    @pl.when(jnp.logical_not(even))
    def _():
        follow(spaced([V_NEW, K_NEW] + v_sinks + k_sinks, [3, 2, 2, 1, 1, 1]))

    @pl.when(t > 0)
    def _():
        counts.wait_recv()

    received(V_OLD)
    received(K_OLD)

    use_sink = flags[0, 0]
    use_window = flags[0, 1]
    held = jnp.where(t >= 2, window, count_in[0:1, :rows])
    allowed = jnp.where(
        lane >= window, use_sink,
        use_window * jnp.where(lane >= FT, (held > 0).astype(jnp.int32),
                               (held >= window).astype(jnp.int32))) > 0

    for h in range(heads):
        s = scores(h, older, allowed)
        top = jnp.maximum(jnp.max(s, axis=1, keepdims=True), own_max[h])
        weight = jnp.exp2(s - top).astype(jnp.bfloat16)
        keep = jnp.exp2(own_max[h] - top)
        denominator = total_of(weight) + own_sum[:, column(h)] * keep
        total = mix(weight, h, older) + own_out[:, column(h)] * keep
        out[:, column(h)] = jnp.where(live_rows, total / denominator, 0.0).astype(jnp.bfloat16)

    @pl.when(has_after)
    def _():
        counts.wait_send()
        for copy in sends.values():
            copy.wait_send()

    for kind, ref in ((V_SINK, v_all), (K_SINK, k_all)):
        for i in range(PIECES):
            along, across = sink_sends(kind, ref, i)
            goes_along, goes_across = sink_goes(kind, i)

            @pl.when(goes_along)
            def _():
                along.wait_send()

            @pl.when(goes_across)
            def _():
                across.wait_send()


def local(spans, heads_axis, queries, keys, values, q_gain, k_gain, frames, flags):
    rows, cols = queries.shape
    heads = cols // HD
    far = pl.BlockSpec(memory_space=pltpu.HBM)
    near = pl.BlockSpec(memory_space=pltpu.VMEM)
    bf16, f32 = jnp.bfloat16, jnp.float32
    held = 2 * rows
    return pl.pallas_call(
        functools.partial(kernel, spans, heads_axis),
        out_shape=pltpu.VMEM((rows, cols), bf16),
        in_specs=[far] * 7,
        out_specs=near,
        scratch_shapes=[
            pltpu.VMEM((cols,), f32),
            pltpu.VMEM((cols,), f32),
            pltpu.SMEM(frames.shape, jnp.int32),
            pltpu.SMEM(flags.shape, jnp.int32),
            pltpu.VMEM((rows, cols), bf16),
            pltpu.VMEM((rows, cols), bf16),
            pltpu.VMEM((rows, cols), bf16),
            pltpu.VMEM((held, cols), bf16),
            pltpu.VMEM((held, cols), bf16),
            pltpu.VMEM((2, rows, HD), f32),
            pltpu.VMEM((2, rows, HD), f32),
            pltpu.VMEM((8, HD), jnp.int32),
            pltpu.VMEM((8, HD), jnp.int32),
            pltpu.VMEM((FT, cols), bf16),
            pltpu.VMEM((FT, cols), bf16),
            pltpu.VMEM((FT, cols), bf16),
            pltpu.VMEM((FT, cols), bf16),
            pltpu.VMEM((heads, rows, 1), f32),
            pltpu.VMEM((rows, cols), f32),
            pltpu.VMEM((rows, cols), f32),
            pltpu.SemaphoreType.DMA((7,)),
            pltpu.SemaphoreType.DMA((COPIES,)),
            pltpu.SemaphoreType.DMA((COPIES,)),
            pltpu.SemaphoreType.DMA((2 * PIECES,)),
        ],
        compiler_params=pltpu.CompilerParams(
            collective_id=0, has_side_effects=True, vmem_limit_bytes=63 * 2**20),
    )(queries, keys, values, q_gain, k_gain, frames, flags)


def solution(mesh):
    placed = (
        P(("groups", "tm"), "head"),
        P(("groups", "tm"), "head"),
        P(("groups", "tm"), "head"),
        P("head"),
        P("head"),
        P(("groups", "tm")),
        P(("groups", "tm"), None),
    )
    return jax.shard_map(
        functools.partial(local, mesh.shape["tm"], mesh.shape["head"]),
        mesh=mesh, in_specs=placed, out_specs=P(("groups", "tm"), "head"), check_vma=False
    )
```

```python
import functools
import math

import jax
import jax.numpy as jnp
from jax import lax
from jax.experimental import pallas as pl
from jax.experimental.pallas import tpu as pltpu
from jax.sharding import PartitionSpec as P

HD = 128
FT = 32
EPSILON = 1e-06
MASKED = -1e30

PIECES = 3
CROSSING = tuple(range(6))
K_ENERGY, Q_ENERGY, COUNT, V_NEW, K_NEW, V_OLD, K_OLD, V_SINK = range(8)
K_SINK = V_SINK + PIECES
COPIES = K_SINK + PIECES


def kernel(spans, heads_axis, q_hbm, k_hbm, v_hbm, q_gain_hbm, k_gain_hbm, frames_hbm, flags_hbm, out,
           q_gain, k_gain, frames, flags, q_raw, k_raw, q_norm, k_all, v_all, energy, energy_in, count, count_in,
           v_new, k_new, v_old, k_old, own_max, own_sum, own_out,
           local_sem, send_sem, recv_sem, hop_sem):
    rows, cols = q_hbm.shape
    heads = cols // HD
    window = 2 * FT
    older, newer, sink = rows, rows + FT, rows + window
    full_width = cols * heads_axis
    t = lax.axis_index("tm")
    even = t % 2 == 0
    side = lax.axis_index("head")

    def column(h):
        return pl.ds(h * HD, HD)

    def load(source, target, index):
        return pltpu.make_async_copy(source, target, local_sem.at[index])

    loads = [load(k_hbm, k_raw, 0), load(v_hbm, v_all.at[pl.ds(0, rows)], 1),
             load(frames_hbm, frames, 2), load(flags_hbm, flags, 3), load(k_gain_hbm, k_gain, 4),
             load(q_hbm, q_raw, 5), load(q_gain_hbm, q_gain, 6)]
    for copy in loads:
        copy.start()

    barrier = pltpu.get_barrier_semaphore()

    def greet(condition, **where):
        @pl.when(condition)
        def _():
            pl.semaphore_signal(barrier, inc=1, device_id=where, device_id_type=pl.DeviceIdType.MESH)

    for other in range(1, heads_axis):
        greet(side >= 0, head=lax.rem(side + other, heads_axis))
    partners = heads_axis - 1
    for step in (-2, -1, 1, 2):
        there = (t + step >= 0) & (t + step < spans)
        greet(there, tm=t + step)
        partners = partners + there.astype(jnp.int32)

    @pl.when(t == 0)
    def _():
        blank = jnp.zeros((window, cols), jnp.bfloat16)
        k_all[pl.ds(older, window)] = blank
        v_all[pl.ds(older, window)] = blank
        count_in[...] = jnp.zeros_like(count_in)

    def remote(kind, source, target, sem=None, **where):
        return pltpu.make_async_remote_copy(
            src_ref=source, dst_ref=target,
            send_sem=send_sem.at[kind] if sem is None else sem, recv_sem=recv_sem.at[kind],
            device_id=where, device_id_type=pl.DeviceIdType.MESH)

    after = {"tm": jnp.minimum(t + 1, spans - 1)}
    hop = {"tm": jnp.minimum(t + 2, spans - 1)}
    has_after = t + 1 < spans
    has_hop = t + 2 < spans

    def squares(ref):
        total = jnp.zeros((rows, HD), jnp.float32)
        for h in range(heads):
            block = ref[:, column(h)].astype(jnp.float32)
            total = total + block * block
        return total

    def piece(i):
        first, last = heads * i // PIECES, heads * (i + 1) // PIECES
        return pl.ds(first * HD, (last - first) * HD)

    def sink_sends(kind, ref, i):
        at = ref.at[pl.ds(sink, FT), piece(i)]
        index = kind - V_SINK + i
        along = remote(kind + i, at, at, sem=hop_sem.at[index], **hop)
        across = remote(kind + i, at, at, **after)
        return along, across

    def sink_goes(kind, i):
        if kind - V_SINK + i in CROSSING:
            return even & has_hop, even & has_after
        return has_hop, (t == 0) & has_after

    def sink_pass(kind, ref, i):
        along, across = sink_sends(kind, ref, i)
        goes_along, goes_across = sink_goes(kind, i)

        @pl.when(goes_along)
        def _():
            along.start()

        @pl.when(goes_across)
        def _():
            across.start()

    def sink_take(kind, ref, i):
        @pl.when(t > 0)
        def _():
            sink_sends(kind, ref, i)[1].wait_recv()
            sink_pass(kind, ref, i)

    def newest(source, target):
        for h in range(heads):
            a, b, c = (source[pl.ds(i * FT, FT), column(h)] for i in range(3))
            target[:, column(h)] = jnp.where(n >= 3 * FT, c, jnp.where(n >= 2 * FT, b, a))

    def second(source, target):
        for h in range(heads):
            a, b = (source[pl.ds(i * FT, FT), column(h)] for i in range(2))
            got = source[pl.ds(newer, FT), column(h)]
            target[:, column(h)] = jnp.where(n >= 3 * FT, b, jnp.where(n >= 2 * FT, a, got))

    counts = remote(COUNT, count, count_in, **after)
    sends = {
        V_NEW: remote(V_NEW, v_new, v_all.at[pl.ds(newer, FT)], **after),
        K_NEW: remote(K_NEW, k_new, k_all.at[pl.ds(newer, FT)], **after),
        V_OLD: remote(V_OLD, v_old, v_all.at[pl.ds(older, FT)], **after),
        K_OLD: remote(K_OLD, k_old, k_all.at[pl.ds(older, FT)], **after),
    }
    shares = [remote(kind, energy.at[kind], energy_in.at[kind], head=lax.rem(side + 1, heads_axis))
              for kind in (K_ENERGY, Q_ENERGY)]

    for copy in loads[:5]:
        copy.wait()
    n = frames[0] * FT
    count[...] = jnp.full(count.shape, n, jnp.int32)
    energy[K_ENERGY] = squares(k_raw)
    newest(v_all, v_new)

    @pl.when(t == 0)
    def _():
        v_all[pl.ds(sink, FT)] = v_all[pl.ds(0, FT)]

    pl.semaphore_wait(barrier, partners)
    shares[K_ENERGY].start()

    @pl.when(t == 0)
    def _():
        for i in range(PIECES):
            sink_pass(V_SINK, v_all, i)

    @pl.when(has_after)
    def _():
        sends[V_NEW].start()
        counts.start()

    for copy in loads[5:]:
        copy.wait()
    energy[Q_ENERGY] = squares(q_raw)
    shares[Q_ENERGY].start()

    def level(index):
        shares[index].wait()
        total = jnp.sum(energy[index] + energy_in[index], axis=1, keepdims=True)
        return lax.rsqrt(total / full_width + EPSILON)

    k_level = level(K_ENERGY)
    for h in range(heads):
        k_all[pl.ds(0, rows), column(h)] = (
            k_raw[:, column(h)].astype(jnp.float32) * k_level * k_gain[column(h)].reshape(1, HD)
        ).astype(jnp.bfloat16)

    @pl.when(t == 0)
    def _():
        k_all[pl.ds(sink, FT)] = k_all[pl.ds(0, FT)]
        for i in range(PIECES):
            sink_pass(K_SINK, k_all, i)

    newest(k_all, k_new)

    @pl.when(has_after)
    def _():
        sends[K_NEW].start()

    q_level = level(Q_ENERGY)
    for h in range(heads):
        q_norm[:, column(h)] = (
            q_raw[:, column(h)].astype(jnp.float32) * q_level * q_gain[column(h)].reshape(1, HD)
        ).astype(jnp.bfloat16)

    def received(kind):
        @pl.when(t > 0)
        def _():
            sends[kind].wait_recv()

    scaling = math.log2(math.e) / math.sqrt(HD)

    def scores(h, start, allowed):
        products = lax.dot_general(
            q_norm[:, column(h)], k_all[pl.ds(start, rows), column(h)],
            (((1,), (1,)), ((), ())), preferred_element_type=jnp.float32)
        return jnp.where(allowed, products * scaling, MASKED)

    def mix(weight, h, start):
        return jnp.dot(weight, v_all[pl.ds(start, rows), column(h)],
                       preferred_element_type=jnp.float32)

    ones = jnp.ones((rows, HD), jnp.bfloat16)

    def total_of(weight):
        return jnp.dot(weight, ones, preferred_element_type=jnp.float32)

    lane = lax.broadcasted_iota(jnp.int32, (1, rows), 1)
    live_keys = lane < n
    live_rows = lax.broadcasted_iota(jnp.int32, (rows, 1), 0) < n

    def own(h):
        s = scores(h, 0, live_keys)
        top = jnp.max(s, axis=1, keepdims=True)
        weight = jnp.exp2(s - top)
        own_max[h] = top
        weight = weight.astype(jnp.bfloat16)
        own_sum[:, column(h)] = total_of(weight)
        own_out[:, column(h)] = mix(weight, h, 0)

    def hand_on(new, old, ref, scratch):
        received(new)
        second(ref, scratch)

        @pl.when(has_after)
        def _():
            sends[old].start()

    def follow(order):
        done = 0
        for step, (what, ready) in enumerate(order):
            if what == V_NEW:
                hand_on(V_NEW, V_OLD, v_all, v_old)
            elif what == K_NEW:
                hand_on(K_NEW, K_OLD, k_all, k_old)
            elif what < K_SINK:
                sink_take(V_SINK, v_all, what - V_SINK)
            else:
                sink_take(K_SINK, k_all, what - K_SINK)
            for h in range(done, ready):
                own(h)
            done = ready
        assert done == heads

    def spaced(order, counts):
        total = sum(counts)
        return [(what, heads * sum(counts[:i + 1]) // total) for i, what in enumerate(order)]

    v_sinks = [V_SINK + i for i in range(PIECES)]
    k_sinks = [K_SINK + i for i in range(PIECES)]

    @pl.when(even)
    def _():
        follow(spaced(v_sinks + [V_NEW, K_NEW] + k_sinks, [0, 0, 1, 1, 3, 2, 2, 1]))

    @pl.when(jnp.logical_not(even))
    def _():
        follow(spaced([V_NEW, K_NEW] + v_sinks + k_sinks, [3, 2, 1, 1, 1, 1, 1, 0]))

    @pl.when(t > 0)
    def _():
        counts.wait_recv()

    received(V_OLD)
    received(K_OLD)

    use_sink = flags[0, 0]
    use_window = flags[0, 1]
    held = jnp.where(t >= 2, window, count_in[0:1, :rows])
    allowed = jnp.where(
        lane >= window, use_sink,
        use_window * jnp.where(lane >= FT, (held > 0).astype(jnp.int32),
                               (held >= window).astype(jnp.int32))) > 0

    for h in range(heads):
        s = scores(h, older, allowed)
        top = jnp.maximum(jnp.max(s, axis=1, keepdims=True), own_max[h])
        weight = jnp.exp2(s - top).astype(jnp.bfloat16)
        keep = jnp.exp2(own_max[h] - top)
        denominator = total_of(weight) + own_sum[:, column(h)] * keep
        total = mix(weight, h, older) + own_out[:, column(h)] * keep
        out[:, column(h)] = jnp.where(live_rows, total / denominator, 0.0).astype(jnp.bfloat16)

    @pl.when(has_after)
    def _():
        counts.wait_send()
        for copy in sends.values():
            copy.wait_send()

    for kind, ref in ((V_SINK, v_all), (K_SINK, k_all)):
        for i in range(PIECES):
            along, across = sink_sends(kind, ref, i)
            goes_along, goes_across = sink_goes(kind, i)

            @pl.when(goes_along)
            def _():
                along.wait_send()

            @pl.when(goes_across)
            def _():
                across.wait_send()


def local(spans, heads_axis, queries, keys, values, q_gain, k_gain, frames, flags):
    rows, cols = queries.shape
    heads = cols // HD
    far = pl.BlockSpec(memory_space=pltpu.HBM)
    near = pl.BlockSpec(memory_space=pltpu.VMEM)
    bf16, f32 = jnp.bfloat16, jnp.float32
    held = 2 * rows
    return pl.pallas_call(
        functools.partial(kernel, spans, heads_axis),
        out_shape=pltpu.VMEM((rows, cols), bf16),
        in_specs=[far] * 7,
        out_specs=near,
        scratch_shapes=[
            pltpu.VMEM((cols,), f32),
            pltpu.VMEM((cols,), f32),
            pltpu.SMEM(frames.shape, jnp.int32),
            pltpu.SMEM(flags.shape, jnp.int32),
            pltpu.VMEM((rows, cols), bf16),
            pltpu.VMEM((rows, cols), bf16),
            pltpu.VMEM((rows, cols), bf16),
            pltpu.VMEM((held, cols), bf16),
            pltpu.VMEM((held, cols), bf16),
            pltpu.VMEM((2, rows, HD), f32),
            pltpu.VMEM((2, rows, HD), f32),
            pltpu.VMEM((8, HD), jnp.int32),
            pltpu.VMEM((8, HD), jnp.int32),
            pltpu.VMEM((FT, cols), bf16),
            pltpu.VMEM((FT, cols), bf16),
            pltpu.VMEM((FT, cols), bf16),
            pltpu.VMEM((FT, cols), bf16),
            pltpu.VMEM((heads, rows, 1), f32),
            pltpu.VMEM((rows, cols), f32),
            pltpu.VMEM((rows, cols), f32),
            pltpu.SemaphoreType.DMA((7,)),
            pltpu.SemaphoreType.DMA((COPIES,)),
            pltpu.SemaphoreType.DMA((COPIES,)),
            pltpu.SemaphoreType.DMA((2 * PIECES,)),
        ],
        compiler_params=pltpu.CompilerParams(
            collective_id=0, has_side_effects=True, vmem_limit_bytes=63 * 2**20),
    )(queries, keys, values, q_gain, k_gain, frames, flags)


def solution(mesh):
    placed = (
        P(("groups", "tm"), "head"),
        P(("groups", "tm"), "head"),
        P(("groups", "tm"), "head"),
        P("head"),
        P("head"),
        P(("groups", "tm")),
        P(("groups", "tm"), None),
    )
    return jax.shard_map(
        functools.partial(local, mesh.shape["tm"], mesh.shape["head"]),
        mesh=mesh, in_specs=placed, out_specs=P(("groups", "tm"), "head"), check_vma=False
    )
```
